1024 devices in a mesh: region: 64 (over z_lo, x), member: 16 (over z_hi, y, core).
Axes of the slice: x: 4, y: 4, z: 32 (z_hi: 2, z_lo: 16; z = z_hi * 16 + z_lo), core: 2. Of those that a mesh axis runs over, the one named last changes fastest.
Arguments:
- members: float32 [256, 1024, 1024], P('member', 'region'), may hold values from -6 to 6
- obs_value: float32 [1024, 1024], P('region'), may hold values from -6 to 6
- obs_precision: float32 [1024, 1024], P('region'), may hold values from 0.02 to 200
- obs_index: int32 [1024, 1024], P('region'), may hold values from 0 to 1023, as said below
- obs_count: int32 [1024], P('region'), may hold values from 256 to 1024
Outputs:
- analysis: float32 [256, 1024, 1024], P('member', 'region')
The draws below stay inside these ranges and needn't reach their ends.
Inputs may be any that keep to these rules, and one draw needn't show every extreme that they name: `obs_count`: slots of a tile from its count onward are empty. `obs_index`: position within its own tile.
All inputs are finite; a program needn't handle non-finite values.
Results may differ from the reference program's by a relative error of at most 0.0005.
Values sent between devices are 32-bit elements; how exact they have to be, the bound alone decides.
No kernel may reach another device: no remote copies, remote signals or barrier semaphores. Data moves between devices by JAX's collectives and lax.ppermute only.
A program may use at most 32 MiB of HBM per device.

```python
import math
import jax
import jax.numpy as jnp
from jax import lax

K = 256
TILE = 1024
OBS = 1024
TILES_DEV = 16
ITERS = 12
TILES = 1024
N_REGION = 64


def draw_obs_index(key, part):
    hot_key = jax.random.fold_in(key, 11)
    pick_key = jax.random.fold_in(key, 12)
    wide_key = jax.random.fold_in(key, 13)
    centres = jax.random.randint(hot_key, (TILES, 4), 0, TILE, dtype=jnp.int32)
    selector = jax.random.randint(pick_key, (TILES, OBS), 0, 4, dtype=jnp.int32)
    spread = jax.random.randint(wide_key, (TILES, OBS), 0, TILE, dtype=jnp.int32)
    repeated = jnp.take_along_axis(centres, selector, axis=1)
    slot_ids = jnp.arange(OBS, dtype=jnp.int32)[None, :]
    return jnp.where(slot_ids < OBS // 8, repeated, spread).astype(jnp.int32)


def draw_obs_precision(key, part):
    low_key = jax.random.fold_in(key, 21)
    high_key = jax.random.fold_in(key, 22)
    background = jnp.exp(jax.random.uniform(low_key, (TILES, OBS), jnp.float32, math.log(0.02), math.log(2.0)))
    background = jnp.clip(background, 0.02, 2.0)
    precise = jnp.exp(jax.random.uniform(high_key, (TILES, OBS), jnp.float32, math.log(40.0), math.log(200.0)))
    precise = jnp.clip(precise, 40.0, 200.0)
    slot_ids = jnp.arange(OBS, dtype=jnp.int32)[None, :]
    return jnp.where(slot_ids < OBS // 8, precise, background).astype(jnp.float32)


def place_ends(values, stream_key, low, largest):
    spot = [jax.random.randint(jax.random.fold_in(stream_key, axis), (), 0, length) for axis, length in enumerate(values.shape)]
    main_axis = values.shape.index(max(values.shape))
    beside = spot[:main_axis] + [(spot[main_axis] + 1) % values.shape[main_axis]] + spot[main_axis + 1:]
    return values.at[tuple(spot)].set(low).at[tuple(beside)].set(largest)


def block_scale(key, shape, cuts, smallest, largest):
    loudness, own = 1.0, jax.random.fold_in(key, 6)
    for dim, shards_of in cuts:
        draws = jnp.exp(jax.random.uniform(jax.random.fold_in(own, dim), (shards_of,), jnp.float32, smallest / len(cuts), largest / len(cuts)))
        loudness = loudness * jnp.repeat(draws, shape[dim] // shards_of).reshape([-1 if axis == dim else 1 for axis in range(len(shape))])
    return loudness


def gaussian(key, dims, scale, most, cuts=(), held_as=jnp.bfloat16):
    values = scale * jax.random.normal(key, dims, jnp.float32)
    if cuts:
        values = values * block_scale(key, dims, cuts, -0.22, 0.18)
    return jnp.clip(values, -most, most).astype(held_as)


def setup_inputs(seed: int = 0) -> dict:
    keys = jax.random.split(jax.random.key(seed), 6)
    members = gaussian(keys[0], (K, TILES, TILE), 1.0, 6.0, ((0, 16), (1, 64)), jnp.float32)
    obs_value = gaussian(keys[1], (TILES, OBS), 1.0, 6.0, ((0, 64),), jnp.float32)
    obs_precision = draw_obs_precision(jax.random.fold_in(keys[5], 71), 0)
    obs_index = draw_obs_index(jax.random.fold_in(keys[5], 71), 0)
    obs_count = place_ends(jax.random.randint(keys[4], (TILES,), OBS // 4, OBS + 1), jax.random.fold_in(keys[4], 1), OBS // 4, OBS).astype(jnp.int32)
    return dict(members=members, obs_value=obs_value, obs_precision=obs_precision, obs_index=obs_index, obs_count=obs_count)


def observe(states, places, observed, accuracy, filled):
    average = lax.optimization_barrier(jnp.sum(states, axis=0)) / K
    deviation = states - average[None]
    sampled = jnp.take_along_axis(deviation, places[None], axis=2)
    baseline = jnp.take_along_axis(average, places, axis=1)
    slot_ids = jnp.arange(places.shape[1], dtype=jnp.int32)
    active = slot_ids[None, :] < filled[:, None]
    weight_root = jnp.where(active, jnp.sqrt(accuracy), jnp.float32(0.0))
    scaled = sampled * weight_root[None]
    innov_row = (weight_root * (observed - baseline))[None]
    stacked = jnp.concatenate([scaled, innov_row], axis=0)
    return (average, deviation, stacked)

def outer_gram(stacked):
    return jnp.einsum('ibo,jbo->bij', stacked, stacked, precision=lax.Precision.HIGHEST)

def transform_weights(gram_matrix):
    ensemble = gram_matrix.shape[1] - 1
    identity = jnp.eye(ensemble, dtype=jnp.float32)
    system = (ensemble - 1.0) * identity + gram_matrix[:, :ensemble, :ensemble]
    right_side = gram_matrix[:, :ensemble, ensemble]
    factor = jnp.sqrt(lax.optimization_barrier(jnp.sum(system * system, axis=(1, 2))) + 1e-06)
    root_iter = system / factor[:, None, None]
    inverse_iter = jnp.broadcast_to(identity, system.shape)

    def one_sweep(sweep_no, iterates):
        root_now, inverse_now = iterates
        middle = 3.0 * identity - jnp.einsum('bij,bjk->bik', inverse_now, root_now, precision=lax.Precision.HIGHEST)
        root_next = 0.5 * jnp.einsum('bij,bjk->bik', root_now, middle, precision=lax.Precision.HIGHEST)
        inverse_next = 0.5 * jnp.einsum('bij,bjk->bik', middle, inverse_now, precision=lax.Precision.HIGHEST)
        return (root_next, inverse_next)
    root_iter, inverse_iter = lax.fori_loop(0, ITERS, one_sweep, (root_iter, inverse_iter))
    inverse_root = inverse_iter / jnp.sqrt(factor)[:, None, None]
    pulled = jnp.einsum('bij,bj->bi', inverse_root, right_side, precision=lax.Precision.HIGHEST)
    shifted = jnp.einsum('bij,bj->bi', inverse_root, pulled, precision=lax.Precision.HIGHEST)
    return math.sqrt(ensemble - 1.0) * inverse_root + shifted[:, :, None]

def analyse(average, deviation, gram_matrix):
    weights = transform_weights(gram_matrix)
    return average[None] + jnp.einsum('jbc,bjk->kbc', deviation, weights, precision=lax.Precision.HIGHEST)

def reference(members, obs_value, obs_precision, obs_index, obs_count):
    columns = members.reshape(K, N_REGION, TILES_DEV, TILE).transpose(1, 0, 2, 3)
    obs_values = obs_value.reshape(N_REGION, TILES_DEV, OBS)
    accuracies = obs_precision.reshape(N_REGION, TILES_DEV, OBS)
    indices = obs_index.reshape(N_REGION, TILES_DEV, OBS)
    obs_counts = obs_count.reshape(N_REGION, TILES_DEV)

    def gram_of(entries):
        states, places, observed, accuracy, filled = entries
        return outer_gram(observe(states, places, observed, accuracy, filled)[2])
    gram_tiles = lax.map(gram_of, (columns, indices, obs_values, accuracies, obs_counts))
    combined = gram_tiles + 0.5 * (jnp.roll(gram_tiles, 1, axis=0) + jnp.roll(gram_tiles, -1, axis=0))

    def analyse_column(entries):
        states, places, observed, accuracy, filled, gram_matrix = entries
        average, deviation, stacked = observe(states, places, observed, accuracy, filled)
        return analyse(average, deviation, gram_matrix)
    result = lax.map(analyse_column, (columns, indices, obs_values, accuracies, obs_counts, combined))
    return result.transpose(1, 0, 2, 3).reshape(K, N_REGION * TILES_DEV, TILE)
```

```python
import functools
import math

import jax
import jax.numpy as jnp
from jax import lax
from jax.experimental import pallas as pl
from jax.experimental.pallas import tpu as pltpu
from jax.sharding import Mesh
from jax.sharding import PartitionSpec as P

K = 256
ITERS = 12
HALF = K // 2
MEMBER = ("zh", "y", "core")
HIGHEST = lax.Precision.HIGHEST
VMEM = pl.BlockSpec(memory_space=pltpu.VMEM)
SMEM = pl.BlockSpec(memory_space=pltpu.SMEM)


def call(kernel, outs, specs, scratch=()):
    return pl.pallas_call(
        kernel,
        out_shape=outs,
        in_specs=specs,
        out_specs=jax.tree.map(lambda _: VMEM, outs),
        scratch_shapes=list(scratch),
        compiler_params=pltpu.CompilerParams(vmem_limit_bytes=24 << 20),
        cost_estimate=pl.CostEstimate(flops=0, bytes_accessed=0, transcendentals=0),
    )


def after(x, token):
    any_space = pl.BlockSpec(memory_space=pl.ANY)
    return pl.pallas_call(
        lambda token_ref, x_ref, out_ref: None,
        out_shape=f32(*x.shape),
        in_specs=[any_space] * 2,
        out_specs=any_space,
        input_output_aliases={1: 0},
    )(token, x)


def f32(*shape):
    return jax.ShapeDtypeStruct(shape, jnp.float32)


def split_kernel(zh_ref, x_ref, first_ref, own_ref, later_ref):
    def rows(band):
        return x_ref[:, band, :]

    for side in range(2):

        @pl.when(zh_ref[0] == side)
        def _():
            mine, theirs = 8 * side, 8 * (1 - side)
            for y in range(4):
                first_ref[pl.ds(16 * y, 16), :] = rows(theirs + 2 * y)
                later_ref[pl.ds(16 * y, 16), :] = rows(theirs + 2 * y + 1)
            for b in range(8):
                own_ref[pl.ds(16 * b, 16), :] = rows(mine + b)


def join_kernel(zh_ref, own_ref, back_ref, out_ref):
    for side in range(2):

        @pl.when(zh_ref[0] == side)
        def _():
            for b in range(8):
                out_ref[:, 8 * side + b, :] = own_ref[pl.ds(16 * b, 16), :]
                out_ref[:, 8 * (1 - side) + b, :] = back_ref[pl.ds(16 * b, 16), :]


def centred(own_ref, other_ref):
    states = jnp.concatenate([own_ref[...], other_ref[...]], axis=0)
    average = jnp.sum(states, axis=0, keepdims=True) / K
    return average, states - average


def product(a, b):
    return jnp.dot(a, b, precision=HIGHEST, preferred_element_type=jnp.float32)


def across(a, b):
    return lax.dot_general(
        a, b, (((1,), (1,)), ((), ())), precision=HIGHEST, preferred_element_type=jnp.float32
    )


def gram_kernel(on_ref, table_ref, own_ref, other_ref, gram_ref):
    @pl.when(on_ref[0] == 1)
    def _():
        average, deviation = centred(own_ref, other_ref)
        weight, pull = table_ref[0:1, :], table_ref[1:2, :]
        scaled = deviation * jnp.sqrt(weight)
        gram = across(scaled, scaled)
        right = across(jnp.broadcast_to(pull - weight * average, (8, 1024)), deviation)
        gram_ref[0:128, :] = gram[:HALF, :HALF]
        gram_ref[128:256, :] = gram[:HALF, HALF:]
        gram_ref[256:384, :] = gram[HALF:, HALF:]
        gram_ref[384:392, :] = right[:, :HALF]
        gram_ref[392:400, :] = right[:, HALF:]


def two_parts(x):
    high = x.astype(jnp.bfloat16)
    return high, (x - high.astype(jnp.float32)).astype(jnp.bfloat16)


def product3(a, b):
    (ah, al), (bh, bl) = two_parts(a), two_parts(b)
    dot = functools.partial(jnp.dot, preferred_element_type=jnp.float32)
    return dot(ah, bh) + (dot(ah, bl) + dot(al, bh))


def analyse_kernel(
    on_ref, gram_ref, west_ref, east_ref, own_ref, other_ref, mine_ref, theirs_ref, u_ref, z_ref
):
    @pl.when(on_ref[0] == 1)
    def _():
        total = gram_ref[...] + 0.5 * (west_ref[...] + east_ref[...])
        g11, g12, g22 = total[:128], total[128:256], total[256:384]
        right = jnp.concatenate([total[384:385], total[392:393]], axis=1)
        gram = jnp.concatenate(
            [jnp.concatenate([g11, g12], axis=1), jnp.concatenate([g12.T, g22], axis=1)], axis=0
        )
        rows = lax.broadcasted_iota(jnp.int32, (K, K), 0)
        columns = lax.broadcasted_iota(jnp.int32, (K, K), 1)
        diagonal = rows == columns
        system = gram + jnp.where(diagonal, K - 1.0, 0.0)
        factor = jnp.sqrt(jnp.sum(system * system, keepdims=True) + 1e-06)
        three = jnp.where(diagonal, 3.0, 0.0)
        root = system / factor
        middle = three - root
        u_ref[...] = 0.5 * product(root, middle)
        z_ref[...] = 0.5 * middle

        def sweep(_, carry):
            root, inverse = u_ref[...], z_ref[...]
            middle = three - product(inverse, root)
            u_ref[...] = 0.5 * product(root, middle)
            z_ref[...] = 0.5 * product(middle, inverse)
            return carry

        lax.fori_loop(0, ITERS - 2, sweep, 0)
        root, inverse = u_ref[...], z_ref[...]
        inverse = 0.5 * product(three - product(inverse, root), inverse)
        inverse = inverse / jnp.sqrt(factor)
        pulled = jnp.sum(inverse * right, axis=1, keepdims=True)
        shift = jnp.sum(inverse * pulled, axis=0, keepdims=True)
        weights = math.sqrt(K - 1.0) * inverse + shift
        average, deviation = centred(own_ref, other_ref)
        result = average + product3(weights, deviation)
        mine_ref[...] = result[:HALF]
        for part in range(8):
            core, y = part // 4, part % 4
            theirs_ref[pl.ds(16 * (2 * y + core), 16), :] = result[HALF + 16 * part : HALF + 16 * part + 16]


def shards(members, obs_value, obs_precision, obs_index, obs_count):
    zh, y, core = (lax.axis_index(a) for a in MEMBER)
    regions = lax.axis_size("region")
    width = members.shape[2]
    side = zh.astype(jnp.int32).reshape(1)
    on = [(core == s).astype(jnp.int32).reshape(1) for s in range(2)]

    first, own, later = call(
        split_kernel, (f32(64, width), f32(128, width), f32(64, width)), [SMEM, VMEM]
    )(side, members)

    def swap(x):
        return lax.ppermute(x, "zh", [(0, 1), (1, 0)])

    def swap_on(x, s):
        return lax.ppermute(x, ("zh", "core"), [(s, 2 + s), (2 + s, s)])

    def to_core(x, s):
        return lax.ppermute(x, "core", [(1 - s, s)])

    def over_y(x):
        return lax.all_to_all(x, "y", split_axis=0, concat_axis=0, tiled=True)

    def over_y_core(x):
        return lax.all_to_all(x, ("y", "core"), split_axis=0, concat_axis=0, tiled=True)

    def beside(x, s):
        found = []
        for odd in (0, 1):
            pairs = []
            for r in range(odd, regions, 2):
                ahead = (r + 1) % regions
                pairs += [(2 * r + s, 2 * ahead + s), (2 * ahead + s, 2 * r + s)]
            found.append(lax.ppermute(x, ("region", "core"), pairs))
        return found

    crossed = swap(first)
    always = obs_count[0] > 0

    def spread(later, own):
        near = over_y(later)
        far = to_core(near, 1)
        return jnp.concatenate([far, near]).reshape(HALF, width)

    def no_spread(later, own):
        return own.reshape(HALF, width)

    later = lax.cond(always, spread, no_spread, later, own)
    later_crossed = swap_on(later, 1)

    band = zh * 8 + y * 2 + core
    pick = lambda t: lax.dynamic_index_in_dim(t, band, 0, keepdims=False)
    places, observed, accuracy, filled = map(pick, (obs_index, obs_value, obs_precision, obs_count))
    slots = jnp.arange(width, dtype=jnp.int32)
    accuracy = jnp.where(slots < filled, accuracy, 0.0)
    hit = places[:, None] == slots[None, :]
    weight = jnp.sum(jnp.where(hit, accuracy[:, None], 0.0), axis=0)
    pull = jnp.sum(jnp.where(hit, (accuracy * observed)[:, None], 0.0), axis=0)
    table = jnp.stack([weight, pull])

    def analysed(s, own, table, other):
        gram = call(gram_kernel, f32(400, 128), [SMEM] + [VMEM] * 3)(
            on[s], table, own, other
        )
        west, east = beside(gram, s)
        return east, call(
            analyse_kernel,
            (f32(HALF, width), f32(HALF, width)),
            [SMEM] + [VMEM] * 5,
            scratch=[pltpu.VMEM((K, K), jnp.float32)] * 2,
        )(on[s], gram, west, east, own, other)

    def first_half(crossed, own, table):
        near = over_y(crossed)
        far = to_core(near, 0)
        return analysed(0, own, table, jnp.concatenate([near, far]).reshape(HALF, width))[1]

    def no_half(crossed, own, table):
        return jnp.zeros_like(own.reshape(HALF, width)), jnp.zeros_like(own.reshape(HALF, width))

    own = lax.cond(always, over_y_core, lambda x: x, own)
    crossed, own, table = lax.optimization_barrier((crossed, own, table))
    mine_0, theirs_0 = lax.cond(always, first_half, no_half, crossed, own, table)
    later_crossed, mine_0 = lax.optimization_barrier((later_crossed, mine_0))
    east, (mine_1, theirs_1) = analysed(1, own, table, later_crossed)
    pairs = [(2 * r + 1, 2 * r) for r in range(regions) if r % 4 in (0, 3)]
    gone = lax.ppermute(east[:8], ("region", "core"), pairs)
    theirs_0 = after(theirs_0, gone)
    back_0 = swap_on(theirs_0, 0)
    back_1 = swap_on(theirs_1, 1)
    mine = over_y_core(jnp.where(core == 0, mine_0, mine_1))
    back_0, mine = lax.optimization_barrier((back_0, mine))
    back = over_y_core(jnp.where(core == 0, back_0, back_1))
    return call(join_kernel, f32(*members.shape), [SMEM] + [VMEM] * 2)(side, mine, back)


def solution(mesh):
    split = Mesh(
        mesh.devices.reshape(mesh.shape["region"], 2, 4, 2), ("region", "zh", "y", "core")
    )
    placed = (
        P(MEMBER, "region", None),
        P("region", None),
        P("region", None),
        P("region", None),
        P("region"),
    )
    return jax.shard_map(
        shards, mesh=split, in_specs=placed, out_specs=P(MEMBER, "region", None), check_vma=False
    )
```

```python
import functools
import math

import jax
import jax.numpy as jnp
from jax import lax
from jax.experimental import pallas as pl
from jax.experimental.pallas import tpu as pltpu
from jax.sharding import Mesh
from jax.sharding import PartitionSpec as P

K = 256
ITERS = 12
HALF = K // 2
MEMBER = ("zh", "y", "core")
HIGHEST = lax.Precision.HIGHEST
VMEM = pl.BlockSpec(memory_space=pltpu.VMEM)
SMEM = pl.BlockSpec(memory_space=pltpu.SMEM)


def call(kernel, outs, specs, scratch=()):
    return pl.pallas_call(
        kernel,
        out_shape=outs,
        in_specs=specs,
        out_specs=jax.tree.map(lambda _: VMEM, outs),
        scratch_shapes=list(scratch),
        compiler_params=pltpu.CompilerParams(vmem_limit_bytes=24 << 20),
        cost_estimate=pl.CostEstimate(flops=0, bytes_accessed=0, transcendentals=0),
    )


def after(x, token):
    any_space = pl.BlockSpec(memory_space=pl.ANY)
    return pl.pallas_call(
        lambda token_ref, x_ref, out_ref: None,
        out_shape=f32(*x.shape),
        in_specs=[VMEM, any_space],
        out_specs=any_space,
        input_output_aliases={1: 0},
    )(token, x)


def f32(*shape):
    return jax.ShapeDtypeStruct(shape, jnp.float32)


def split_kernel(zh_ref, x_ref, first_ref, own_ref, later_ref):
    def rows(band):
        return x_ref[:, band, :]

    for side in range(2):

        @pl.when(zh_ref[0] == side)
        def _():
            mine, theirs = 8 * side, 8 * (1 - side)
            for y in range(4):
                first_ref[pl.ds(16 * y, 16), :] = rows(theirs + 2 * y)
                later_ref[pl.ds(16 * y, 16), :] = rows(theirs + 2 * y + 1)
            for b in range(8):
                own_ref[pl.ds(16 * b, 16), :] = rows(mine + b)


def join_kernel(zh_ref, own_ref, first_ref, later_ref, out_ref):
    for side in range(2):

        @pl.when(zh_ref[0] == side)
        def _():
            mine, theirs = 8 * side, 8 * (1 - side)
            for b in range(8):
                out_ref[:, mine + b, :] = own_ref[pl.ds(16 * b, 16), :]
            for y in range(4):
                out_ref[:, theirs + 2 * y, :] = first_ref[pl.ds(16 * y, 16), :]
                out_ref[:, theirs + 2 * y + 1, :] = later_ref[pl.ds(16 * y, 16), :]


def centred(own_ref, other_ref):
    states = jnp.concatenate([own_ref[...], other_ref[...]], axis=0)
    average = jnp.sum(states, axis=0, keepdims=True) / K
    return average, states - average


def product(a, b):
    return jnp.dot(a, b, precision=HIGHEST, preferred_element_type=jnp.float32)


def across(a, b):
    return lax.dot_general(
        a, b, (((1,), (1,)), ((), ())), precision=HIGHEST, preferred_element_type=jnp.float32
    )


def gram_kernel(on_ref, table_ref, own_ref, other_ref, gram_ref):
    @pl.when(on_ref[0] == 1)
    def _():
        average, deviation = centred(own_ref, other_ref)
        weight, pull = table_ref[0:1, :], table_ref[1:2, :]
        scaled = deviation * jnp.sqrt(weight)
        gram = across(scaled, scaled)
        right = across(jnp.broadcast_to(pull - weight * average, (8, 1024)), deviation)
        gram_ref[0:128, :] = gram[:HALF, :HALF]
        gram_ref[128:256, :] = gram[:HALF, HALF:]
        gram_ref[256:384, :] = gram[HALF:, HALF:]
        gram_ref[384:392, :] = right[:, :HALF]
        gram_ref[392:400, :] = right[:, HALF:]


def two_parts(x):
    high = x.astype(jnp.bfloat16)
    return high, (x - high.astype(jnp.float32)).astype(jnp.bfloat16)


def product3(a, b):
    (ah, al), (bh, bl) = two_parts(a), two_parts(b)
    dot = functools.partial(jnp.dot, preferred_element_type=jnp.float32)
    return dot(ah, bh) + (dot(ah, bl) + dot(al, bh))


def analyse_kernel(
    on_ref, gram_ref, west_ref, east_ref, own_ref, other_ref, mine_ref, theirs_ref, u_ref, z_ref
):
    @pl.when(on_ref[0] == 1)
    def _():
        total = gram_ref[...] + 0.5 * (west_ref[...] + east_ref[...])
        g11, g12, g22 = total[:128], total[128:256], total[256:384]
        right = jnp.concatenate([total[384:385], total[392:393]], axis=1)
        gram = jnp.concatenate(
            [jnp.concatenate([g11, g12], axis=1), jnp.concatenate([g12.T, g22], axis=1)], axis=0
        )
        rows = lax.broadcasted_iota(jnp.int32, (K, K), 0)
        columns = lax.broadcasted_iota(jnp.int32, (K, K), 1)
        diagonal = rows == columns
        system = gram + jnp.where(diagonal, K - 1.0, 0.0)
        factor = jnp.sqrt(jnp.sum(system * system, keepdims=True) + 1e-06)
        three = jnp.where(diagonal, 3.0, 0.0)
        root = system / factor
        middle = three - root
        u_ref[...] = 0.5 * product(root, middle)
        z_ref[...] = 0.5 * middle

        def sweep(_, carry):
            root, inverse = u_ref[...], z_ref[...]
            middle = three - product(inverse, root)
            u_ref[...] = 0.5 * product(root, middle)
            z_ref[...] = 0.5 * product(middle, inverse)
            return carry

        lax.fori_loop(0, ITERS - 2, sweep, 0)
        root, inverse = u_ref[...], z_ref[...]
        inverse = 0.5 * product(three - product(inverse, root), inverse)
        inverse = inverse / jnp.sqrt(factor)
        pulled = jnp.sum(inverse * right, axis=1, keepdims=True)
        shift = jnp.sum(inverse * pulled, axis=0, keepdims=True)
        weights = math.sqrt(K - 1.0) * inverse + shift
        average, deviation = centred(own_ref, other_ref)
        result = average + product3(weights, deviation)
        mine_ref[...] = result[:HALF]
        theirs_ref[...] = result[HALF:]


def shards(members, obs_value, obs_precision, obs_index, obs_count):
    zh, y, core = (lax.axis_index(a) for a in MEMBER)
    regions = lax.axis_size("region")
    width = members.shape[2]
    side = zh.astype(jnp.int32).reshape(1)
    on = [(core == s).astype(jnp.int32).reshape(1) for s in range(2)]

    first, own, later = call(
        split_kernel, (f32(64, width), f32(128, width), f32(64, width)), [SMEM, VMEM]
    )(side, members)

    def swap(x):
        return lax.ppermute(x, "zh", [(0, 1), (1, 0)])

    def swap_on(x, s):
        return lax.ppermute(x, ("zh", "core"), [(s, 2 + s), (2 + s, s)])

    def to_core(x, s):
        return lax.ppermute(x, "core", [(1 - s, s)])

    def over_y(x):
        return lax.all_to_all(x, "y", split_axis=0, concat_axis=0, tiled=True)

    def over_y_core(x):
        return lax.all_to_all(x, ("y", "core"), split_axis=0, concat_axis=0, tiled=True)

    def beside(x, s):
        found = []
        for odd in (0, 1):
            pairs = []
            for r in range(odd, regions, 2):
                ahead = (r + 1) % regions
                pairs += [(2 * r + s, 2 * ahead + s), (2 * ahead + s, 2 * r + s)]
            found.append(lax.ppermute(x, ("region", "core"), pairs))
        return found

    crossed = swap(first)
    always = obs_count[0] > 0

    def spread(later, own):
        near = over_y(later)
        far = to_core(near, 1)
        return jnp.concatenate([far, near]).reshape(HALF, width)

    def no_spread(later, own):
        return own.reshape(HALF, width)

    later = lax.cond(always, spread, no_spread, later, own)
    later_crossed = swap_on(later, 1)

    band = zh * 8 + y * 2 + core
    pick = lambda t: lax.dynamic_index_in_dim(t, band, 0, keepdims=False)
    places, observed, accuracy, filled = map(pick, (obs_index, obs_value, obs_precision, obs_count))
    slots = jnp.arange(width, dtype=jnp.int32)
    accuracy = jnp.where(slots < filled, accuracy, 0.0)
    hit = places[:, None] == slots[None, :]
    weight = jnp.sum(jnp.where(hit, accuracy[:, None], 0.0), axis=0)
    pull = jnp.sum(jnp.where(hit, (accuracy * observed)[:, None], 0.0), axis=0)
    table = jnp.stack([weight, pull])

    def analysed(s, own, table, other):
        gram = call(gram_kernel, f32(400, 128), [SMEM] + [VMEM] * 3)(
            on[s], table, own, other
        )
        west, east = beside(gram, s)
        return west[:8] + east[:8], call(
            analyse_kernel,
            (f32(HALF, width), f32(HALF, width)),
            [SMEM] + [VMEM] * 5,
            scratch=[pltpu.VMEM((K, K), jnp.float32)] * 2,
        )(on[s], gram, west, east, own, other)

    def first_half(crossed, own, table):
        near = over_y(crossed)
        far = to_core(near, 0)
        return analysed(0, own, table, jnp.concatenate([near, far]).reshape(HALF, width))[1]

    def no_half(crossed, own, table):
        return jnp.zeros_like(own.reshape(HALF, width)), jnp.zeros_like(own.reshape(HALF, width))

    own = lax.cond(always, over_y_core, lambda x: x, own)
    crossed, own, table = lax.optimization_barrier((crossed, own, table))
    mine_0, theirs_0 = lax.cond(always, first_half, no_half, crossed, own, table)
    later_crossed, mine_0 = lax.optimization_barrier((later_crossed, mine_0))
    neighbours, (mine_1, theirs_1) = analysed(1, own, table, later_crossed)
    gone = to_core(neighbours, 0)
    back_0 = swap_on(after(theirs_0, gone), 0)

    def spread_back(theirs, s):
        send, keep = jnp.split(theirs, [64]) if s else jnp.split(theirs, [64])[::-1]
        return over_y(jnp.where(core == s, keep, to_core(send, 1 - s)))

    crossing = lax.cond(always, lambda x: spread_back(x, 1), lambda x: x[:64], theirs_1)
    back_1 = swap(crossing)
    mine = jnp.where(core == 0, mine_0, mine_1)
    mine = lax.cond(always, over_y_core, lambda x: x, mine)
    back_0, mine = lax.optimization_barrier((back_0, mine))
    back_0 = lax.cond(always, lambda x: spread_back(x, 0), lambda x: x[:64], back_0)
    return call(join_kernel, f32(*members.shape), [SMEM] + [VMEM] * 3)(side, mine, back_0, back_1)


def solution(mesh):
    split = Mesh(
        mesh.devices.reshape(mesh.shape["region"], 2, 4, 2), ("region", "zh", "y", "core")
    )
    placed = (
        P(MEMBER, "region", None),
        P("region", None),
        P("region", None),
        P("region", None),
        P("region"),
    )
    return jax.shard_map(
        shards, mesh=split, in_specs=placed, out_specs=P(MEMBER, "region", None), check_vma=False
    )
```

```python
import functools
import math

import jax
import jax.numpy as jnp
from jax import lax
from jax.experimental import pallas as pl
from jax.experimental.pallas import tpu as pltpu
from jax.sharding import Mesh
from jax.sharding import PartitionSpec as P

K = 256
ITERS = 12
HALF = K // 2
MEMBER = ("zh", "y", "core")
HIGHEST = lax.Precision.HIGHEST
VMEM = pl.BlockSpec(memory_space=pltpu.VMEM)
SMEM = pl.BlockSpec(memory_space=pltpu.SMEM)


def call(kernel, outs, specs, scratch=()):
    return pl.pallas_call(
        kernel,
        out_shape=outs,
        in_specs=specs,
        out_specs=jax.tree.map(lambda _: VMEM, outs),
        scratch_shapes=list(scratch),
        compiler_params=pltpu.CompilerParams(vmem_limit_bytes=24 << 20),
        cost_estimate=pl.CostEstimate(flops=0, bytes_accessed=0, transcendentals=0),
    )


def f32(*shape):
    return jax.ShapeDtypeStruct(shape, jnp.float32)


def split_kernel(zh_ref, x_ref, first_ref, own_ref, later_ref):
    def rows(band):
        return x_ref[:, band, :]

    for side in range(2):

        @pl.when(zh_ref[0] == side)
        def _():
            mine, theirs = 8 * side, 8 * (1 - side)
            for y in range(4):
                first_ref[pl.ds(16 * y, 16), :] = rows(theirs + 2 * y)
                later_ref[pl.ds(16 * y, 16), :] = rows(theirs + 2 * y + 1)
            for b in range(8):
                own_ref[pl.ds(16 * b, 16), :] = rows(mine + b)


def join_kernel(zh_ref, own_ref, first_ref, later_ref, out_ref):
    for side in range(2):

        @pl.when(zh_ref[0] == side)
        def _():
            mine, theirs = 8 * side, 8 * (1 - side)
            for b in range(8):
                out_ref[:, mine + b, :] = own_ref[pl.ds(16 * b, 16), :]
            for y in range(4):
                out_ref[:, theirs + 2 * y, :] = first_ref[pl.ds(16 * y, 16), :]
                out_ref[:, theirs + 2 * y + 1, :] = later_ref[pl.ds(16 * y, 16), :]


def product(a, b):
    return jnp.dot(a, b, precision=HIGHEST, preferred_element_type=jnp.float32)


def across(a, b):
    return lax.dot_general(
        a, b, (((1,), (1,)), ((), ())), precision=HIGHEST, preferred_element_type=jnp.float32
    )


def gram_kernel(core_ref, table_ref, own_ref, early_ref, late_ref, gram_ref, average_ref, deviation_ref):
    other = jnp.where(core_ref[0] == 0, early_ref[...], late_ref[...])
    states = jnp.concatenate([own_ref[...], other], axis=0)
    average = jnp.sum(states, axis=0, keepdims=True) / K
    deviation = states - average
    average_ref[...] = jnp.broadcast_to(average, average_ref.shape)
    deviation_ref[...] = deviation
    weight, pull = table_ref[0:1, :], table_ref[1:2, :]
    scaled = deviation * jnp.sqrt(weight)
    gram = across(scaled, scaled)
    right = across(jnp.broadcast_to(pull - weight * average, average_ref.shape), deviation)
    gram_ref[0:128, :] = gram[:HALF, :HALF]
    gram_ref[128:256, :] = gram[:HALF, HALF:]
    gram_ref[256:384, :] = gram[HALF:, HALF:]
    gram_ref[384:392, :] = right[:, :HALF]
    gram_ref[392:400, :] = right[:, HALF:]


def two_parts(x):
    high = x.astype(jnp.bfloat16)
    return high, (x - high.astype(jnp.float32)).astype(jnp.bfloat16)


def product3(a, b):
    (ah, al), (bh, bl) = two_parts(a), two_parts(b)
    dot = functools.partial(jnp.dot, preferred_element_type=jnp.float32)
    return dot(ah, bh) + (dot(ah, bl) + dot(al, bh))


def analyse_kernel(
    core_ref, gram_ref, west_ref, east_ref, average_ref, deviation_ref, mine_ref, keep_ref, send_ref, u_ref, z_ref
):
    total = gram_ref[...] + 0.5 * (west_ref[...] + east_ref[...])
    g11, g12, g22 = total[:128], total[128:256], total[256:384]
    right = jnp.concatenate([total[384:385], total[392:393]], axis=1)
    gram = jnp.concatenate(
        [jnp.concatenate([g11, g12], axis=1), jnp.concatenate([g12.T, g22], axis=1)], axis=0
    )
    rows = lax.broadcasted_iota(jnp.int32, (K, K), 0)
    columns = lax.broadcasted_iota(jnp.int32, (K, K), 1)
    diagonal = rows == columns
    system = gram + jnp.where(diagonal, K - 1.0, 0.0)
    factor = jnp.sqrt(jnp.sum(system * system, keepdims=True) + 1e-06)
    three = jnp.where(diagonal, 3.0, 0.0)
    root = system / factor
    middle = three - root
    u_ref[...] = 0.5 * product(root, middle)
    z_ref[...] = 0.5 * middle

    def sweep(_, carry):
        root, inverse = u_ref[...], z_ref[...]
        middle = three - product(inverse, root)
        u_ref[...] = 0.5 * product(root, middle)
        z_ref[...] = 0.5 * product(middle, inverse)
        return carry

    lax.fori_loop(0, ITERS - 2, sweep, 0)
    root, inverse = u_ref[...], z_ref[...]
    inverse = 0.5 * product(three - product(inverse, root), inverse)
    inverse = inverse / jnp.sqrt(factor)
    pulled = jnp.sum(inverse * right, axis=1, keepdims=True)
    shift = jnp.sum(inverse * pulled, axis=0, keepdims=True)
    weights = math.sqrt(K - 1.0) * inverse + shift
    result = average_ref[0:1, :] + product3(weights, deviation_ref[...])
    mine_ref[...] = result[:HALF]
    quarter = HALF // 2
    for core in range(2):

        @pl.when(core_ref[0] == core)
        def _():
            keep_ref[...] = result[HALF + core * quarter :][:quarter]
            send_ref[...] = result[HALF + (1 - core) * quarter :][:quarter]


def shards(members, obs_value, obs_precision, obs_index, obs_count):
    zh, y, core = (lax.axis_index(a) for a in MEMBER)
    regions = lax.axis_size("region")
    width = members.shape[2]
    side = zh.astype(jnp.int32).reshape(1)
    which = core.astype(jnp.int32).reshape(1)

    first, own, later = call(
        split_kernel, (f32(64, width), f32(128, width), f32(64, width)), [SMEM, VMEM]
    )(side, members)

    def swap(x):
        return lax.ppermute(x, "zh", [(0, 1), (1, 0)])

    def swap_on(x, s):
        return lax.ppermute(x, ("zh", "core"), [(s, 2 + s), (2 + s, s)])

    def to_core(x, s):
        return lax.ppermute(x, "core", [(1 - s, s)])

    def over_y(x):
        return lax.all_to_all(x, "y", split_axis=0, concat_axis=0, tiled=True)

    def over_y_core(x):
        return lax.all_to_all(x, ("y", "core"), split_axis=0, concat_axis=0, tiled=True)

    def beside(x):
        found = []
        for odd in (0, 1):
            ahead = [(r, (r + 1) % regions) for r in range(odd, regions, 2)]
            found.append(lax.ppermute(x, "region", ahead + [(b, a) for a, b in ahead]))
        return found

    crossed = swap(first)
    always = obs_count[0] > 0

    def spread(later, own):
        near = over_y(later)
        far = to_core(near, 1)
        return jnp.concatenate([far, near]).reshape(HALF, width)

    def no_spread(later, own):
        return own.reshape(HALF, width)

    later = lax.cond(always, spread, no_spread, later, own)
    later_crossed = swap_on(later, 1)

    band = zh * 8 + y * 2 + core
    pick = lambda t: lax.dynamic_index_in_dim(t, band, 0, keepdims=False)
    places, observed, accuracy, filled = map(pick, (obs_index, obs_value, obs_precision, obs_count))
    slots = jnp.arange(width, dtype=jnp.int32)
    accuracy = jnp.where(slots < filled, accuracy, 0.0)
    hit = places[:, None] == slots[None, :]
    weight = jnp.sum(jnp.where(hit, accuracy[:, None], 0.0), axis=0)
    pull = jnp.sum(jnp.where(hit, (accuracy * observed)[:, None], 0.0), axis=0)
    table = jnp.stack([weight, pull])

    def gathered(crossed):
        near = over_y(crossed)
        far = to_core(near, 0)
        return jnp.concatenate([near, far]).reshape(HALF, width)

    own = lax.cond(always, over_y_core, lambda x: x, own)
    crossed, own, table = lax.optimization_barrier((crossed, own, table))
    early = lax.cond(always, gathered, lambda x: jnp.concatenate([x, x]).reshape(HALF, width), crossed)
    later_crossed, early = lax.optimization_barrier((later_crossed, early))

    gram, average, deviation = call(
        gram_kernel, (f32(400, 128), f32(8, width), f32(K, width)), [SMEM] + [VMEM] * 4
    )(which, table, own, early, later_crossed)
    west, east = beside(gram)
    mine, keep, send = call(
        analyse_kernel,
        (f32(HALF, width), f32(64, width), f32(64, width)),
        [SMEM] + [VMEM] * 5,
        scratch=[pltpu.VMEM((K, K), jnp.float32)] * 2,
    )(which, gram, west, east, average, deviation)

    got = lax.ppermute(send, "core", [(0, 1), (1, 0)])
    back_0 = swap(jnp.where(core == 0, keep, got))
    crossing = lax.cond(always, over_y, lambda x: x, jnp.where(core == 0, got, keep))
    back_1 = swap(crossing)
    crossing, mine = lax.optimization_barrier((crossing, mine))
    mine = lax.cond(always, over_y_core, lambda x: x, mine)
    back_0, mine = lax.optimization_barrier((back_0, mine))
    back_0 = lax.cond(always, over_y, lambda x: x, back_0)
    return call(join_kernel, f32(*members.shape), [SMEM] + [VMEM] * 3)(side, mine, back_0, back_1)


def solution(mesh):
    split = Mesh(
        mesh.devices.reshape(mesh.shape["region"], 2, 4, 2), ("region", "zh", "y", "core")
    )
    placed = (
        P(MEMBER, "region", None),
        P("region", None),
        P("region", None),
        P("region", None),
        P("region"),
    )
    return jax.shard_map(
        shards, mesh=split, in_specs=placed, out_specs=P(MEMBER, "region", None), check_vma=False
    )
```

```python
import functools
import math

import jax
import jax.numpy as jnp
from jax import lax
from jax.experimental import pallas as pl
from jax.experimental.pallas import tpu as pltpu
from jax.sharding import Mesh
from jax.sharding import PartitionSpec as P

K = 256
ITERS = 12
HALF = K // 2
MEMBER = ("zh", "y", "core")
HIGHEST = lax.Precision.HIGHEST
VMEM = pl.BlockSpec(memory_space=pltpu.VMEM)
SMEM = pl.BlockSpec(memory_space=pltpu.SMEM)


def call(kernel, outs, specs, scratch=()):
    return pl.pallas_call(
        kernel,
        out_shape=outs,
        in_specs=specs,
        out_specs=jax.tree.map(lambda _: VMEM, outs),
        scratch_shapes=list(scratch),
        compiler_params=pltpu.CompilerParams(vmem_limit_bytes=24 << 20),
        cost_estimate=pl.CostEstimate(flops=0, bytes_accessed=0, transcendentals=0),
    )


def f32(*shape):
    return jax.ShapeDtypeStruct(shape, jnp.float32)


def split_kernel(zh_ref, x_ref, first_ref, own_ref, later_ref):
    def rows(band):
        return x_ref[:, band, :]

    for side in range(2):

        @pl.when(zh_ref[0] == side)
        def _():
            mine, theirs = 8 * side, 8 * (1 - side)
            for y in range(4):
                first_ref[pl.ds(16 * y, 16), :] = rows(theirs + 2 * y)
                later_ref[pl.ds(16 * y, 16), :] = rows(theirs + 2 * y + 1)
            for b in range(8):
                own_ref[pl.ds(16 * b, 16), :] = rows(mine + b)


def join_kernel(zh_ref, own_ref, a_ref, b_ref, c_ref, d_ref, out_ref):
    for side in range(2):

        @pl.when(zh_ref[0] == side)
        def _():
            mine, theirs = 8 * side, 8 * (1 - side)
            for b in range(8):
                out_ref[:, mine + b, :] = own_ref[pl.ds(16 * b, 16), :]
            for y in range(4):
                out_ref[0:8, theirs + 2 * y, :] = a_ref[y]
                out_ref[8:16, theirs + 2 * y, :] = b_ref[y]
                out_ref[0:8, theirs + 2 * y + 1, :] = c_ref[y]
                out_ref[8:16, theirs + 2 * y + 1, :] = d_ref[y]


def product(a, b):
    return jnp.dot(a, b, precision=HIGHEST, preferred_element_type=jnp.float32)


def across(a, b):
    return lax.dot_general(
        a, b, (((1,), (1,)), ((), ())), precision=HIGHEST, preferred_element_type=jnp.float32
    )


def gram_kernel(core_ref, table_ref, own_ref, early_ref, late_ref, gram_ref, average_ref, deviation_ref):
    other = jnp.where(core_ref[0] == 0, early_ref[...], late_ref[...])
    states = jnp.concatenate([own_ref[...], other], axis=0)
    average = jnp.sum(states, axis=0, keepdims=True) / K
    deviation = states - average
    average_ref[...] = jnp.broadcast_to(average, average_ref.shape)
    deviation_ref[...] = deviation
    weight, pull = table_ref[0:1, :], table_ref[1:2, :]
    scaled = deviation * jnp.sqrt(weight)
    gram = across(scaled, scaled)
    right = across(jnp.broadcast_to(pull - weight * average, average_ref.shape), deviation)
    gram_ref[0:128, :] = gram[:HALF, :HALF]
    gram_ref[128:256, :] = gram[:HALF, HALF:]
    gram_ref[256:384, :] = gram[HALF:, HALF:]
    gram_ref[384:392, :] = right[:, :HALF]
    gram_ref[392:400, :] = right[:, HALF:]


def two_parts(x):
    high = x.astype(jnp.bfloat16)
    return high, (x - high.astype(jnp.float32)).astype(jnp.bfloat16)


def product3(a, b):
    (ah, al), (bh, bl) = two_parts(a), two_parts(b)
    dot = functools.partial(jnp.dot, preferred_element_type=jnp.float32)
    return dot(ah, bh) + (dot(ah, bl) + dot(al, bh))


def analyse_kernel(
    core_ref, gram_ref, west_ref, east_ref, average_ref, deviation_ref, mine_ref, keep_ref, send_ref, u_ref, z_ref
):
    total = gram_ref[...] + 0.5 * (west_ref[...] + east_ref[...])
    g11, g12, g22 = total[:128], total[128:256], total[256:384]
    right = jnp.concatenate([total[384:385], total[392:393]], axis=1)
    gram = jnp.concatenate(
        [jnp.concatenate([g11, g12], axis=1), jnp.concatenate([g12.T, g22], axis=1)], axis=0
    )
    rows = lax.broadcasted_iota(jnp.int32, (K, K), 0)
    columns = lax.broadcasted_iota(jnp.int32, (K, K), 1)
    diagonal = rows == columns
    system = gram + jnp.where(diagonal, K - 1.0, 0.0)
    factor = jnp.sqrt(jnp.sum(system * system, keepdims=True) + 1e-06)
    three = jnp.where(diagonal, 3.0, 0.0)
    root = system / factor
    middle = three - root
    u_ref[...] = 0.5 * product(root, middle)
    z_ref[...] = 0.5 * middle

    def sweep(_, carry):
        root, inverse = u_ref[...], z_ref[...]
        middle = three - product(inverse, root)
        u_ref[...] = 0.5 * product(root, middle)
        z_ref[...] = 0.5 * product(middle, inverse)
        return carry

    lax.fori_loop(0, ITERS - 2, sweep, 0)
    root, inverse = u_ref[...], z_ref[...]
    inverse = 0.5 * product(three - product(inverse, root), inverse)
    inverse = inverse / jnp.sqrt(factor)
    pulled = jnp.sum(inverse * right, axis=1, keepdims=True)
    shift = jnp.sum(inverse * pulled, axis=0, keepdims=True)
    weights = math.sqrt(K - 1.0) * inverse + shift
    result = average_ref[0:1, :] + product3(weights, deviation_ref[...])
    mine_ref[...] = result[:HALF]
    quarter = HALF // 2
    for core in range(2):

        @pl.when(core_ref[0] == core)
        def _():
            keep_ref[...] = result[HALF + core * quarter :][:quarter]
            send_ref[...] = result[HALF + (1 - core) * quarter :][:quarter]


def shards(members, obs_value, obs_precision, obs_index, obs_count):
    zh, y, core = (lax.axis_index(a) for a in MEMBER)
    regions = lax.axis_size("region")
    width = members.shape[2]
    side = zh.astype(jnp.int32).reshape(1)
    which = core.astype(jnp.int32).reshape(1)

    first, own, later = call(
        split_kernel, (f32(64, width), f32(128, width), f32(64, width)), [SMEM, VMEM]
    )(side, members)

    def swap(x):
        return lax.ppermute(x, "zh", [(0, 1), (1, 0)])

    def swap_on(x, s):
        return lax.ppermute(x, ("zh", "core"), [(s, 2 + s), (2 + s, s)])

    def to_core(x, s):
        return lax.ppermute(x, "core", [(1 - s, s)])

    def over_y(x):
        return lax.all_to_all(x, "y", split_axis=0, concat_axis=0, tiled=True)

    def over_y_core(x):
        return lax.all_to_all(x, ("y", "core"), split_axis=0, concat_axis=0, tiled=True)

    def beside(x):
        found = []
        for odd in (0, 1):
            ahead = [(r, (r + 1) % regions) for r in range(odd, regions, 2)]
            found.append(lax.ppermute(x, "region", ahead + [(b, a) for a, b in ahead]))
        return found

    crossed = swap(first)
    always = obs_count[0] > 0

    def spread(later, own):
        near = over_y(later)
        far = to_core(near, 1)
        return jnp.concatenate([far, near]).reshape(HALF, width)

    def no_spread(later, own):
        return own.reshape(HALF, width)

    later = lax.cond(always, spread, no_spread, later, own)
    later_crossed = swap_on(later, 1)

    band = zh * 8 + y * 2 + core
    pick = lambda t: lax.dynamic_index_in_dim(t, band, 0, keepdims=False)
    places, observed, accuracy, filled = map(pick, (obs_index, obs_value, obs_precision, obs_count))
    slots = jnp.arange(width, dtype=jnp.int32)
    accuracy = jnp.where(slots < filled, accuracy, 0.0)
    hit = places[:, None] == slots[None, :]
    weight = jnp.sum(jnp.where(hit, accuracy[:, None], 0.0), axis=0)
    pull = jnp.sum(jnp.where(hit, (accuracy * observed)[:, None], 0.0), axis=0)
    table = jnp.stack([weight, pull])

    def gathered(crossed):
        near = over_y(crossed)
        far = to_core(near, 0)
        return jnp.concatenate([near, far]).reshape(HALF, width)

    own = lax.cond(always, over_y_core, lambda x: x, own)
    crossed, own, table = lax.optimization_barrier((crossed, own, table))
    early = lax.cond(always, gathered, lambda x: jnp.concatenate([x, x]).reshape(HALF, width), crossed)
    later_crossed, early = lax.optimization_barrier((later_crossed, early))

    gram, average, deviation = call(
        gram_kernel, (f32(400, 128), f32(8, width), f32(K, width)), [SMEM] + [VMEM] * 4
    )(which, table, own, early, later_crossed)
    west, east = beside(gram)
    mine, keep, send = call(
        analyse_kernel,
        (f32(HALF, width), f32(64, width), f32(64, width)),
        [SMEM] + [VMEM] * 5,
        scratch=[pltpu.VMEM((K, K), jnp.float32)] * 2,
    )(which, gram, west, east, average, deviation)

    got = lax.ppermute(send, "core", [(0, 1), (1, 0)])
    lower = jnp.where(core == 0, keep, got).reshape(4, 16, width)
    upper = jnp.where(core == 0, got, keep).reshape(4, 16, width)
    back_0 = swap(lower[:, :8])
    crossing = lax.cond(
        always,
        lambda x, y: over_y(jnp.concatenate([x, y], axis=1)),
        lambda x, y: jnp.concatenate([y, x], axis=1),
        lower[:, 8:],
        upper,
    )
    rest = [swap(crossing[:, 8 * k : 8 * k + 8]) for k in range(3)]
    crossing, mine = lax.optimization_barrier((crossing, mine))
    mine = lax.cond(always, over_y_core, lambda x: x, mine)
    back_0, mine = lax.optimization_barrier((back_0, mine))
    back_0 = lax.cond(always, over_y, lambda x: x, back_0)
    return call(join_kernel, f32(*members.shape), [SMEM] + [VMEM] * 5)(side, mine, back_0, *rest)


def solution(mesh):
    split = Mesh(
        mesh.devices.reshape(mesh.shape["region"], 2, 4, 2), ("region", "zh", "y", "core")
    )
    placed = (
        P(MEMBER, "region", None),
        P("region", None),
        P("region", None),
        P("region", None),
        P("region"),
    )
    return jax.shard_map(
        shards, mesh=split, in_specs=placed, out_specs=P(MEMBER, "region", None), check_vma=False
    )
```

```python
import functools
import math

import jax
import jax.numpy as jnp
from jax import lax
from jax.experimental import pallas as pl
from jax.experimental.pallas import tpu as pltpu
from jax.sharding import Mesh
from jax.sharding import PartitionSpec as P

K = 256
ITERS = 12
HALF = K // 2
MEMBER = ("zh", "y", "core")
HIGHEST = lax.Precision.HIGHEST
VMEM = pl.BlockSpec(memory_space=pltpu.VMEM)
SMEM = pl.BlockSpec(memory_space=pltpu.SMEM)


def call(kernel, outs, specs, scratch=()):
    return pl.pallas_call(
        kernel,
        out_shape=outs,
        in_specs=specs,
        out_specs=jax.tree.map(lambda _: VMEM, outs),
        scratch_shapes=list(scratch),
        compiler_params=pltpu.CompilerParams(vmem_limit_bytes=24 << 20),
        cost_estimate=pl.CostEstimate(flops=0, bytes_accessed=0, transcendentals=0),
    )


def f32(*shape):
    return jax.ShapeDtypeStruct(shape, jnp.float32)


def split_kernel(zh_ref, x_ref, first_ref, own_ref, later_ref):
    def rows(band):
        return x_ref[:, band, :]

    for side in range(2):

        @pl.when(zh_ref[0] == side)
        def _():
            mine, theirs = 8 * side, 8 * (1 - side)
            for y in range(4):
                first_ref[pl.ds(16 * y, 16), :] = rows(theirs + 2 * y)
                later_ref[pl.ds(16 * y, 16), :] = rows(theirs + 2 * y + 1)
            for b in range(8):
                own_ref[pl.ds(16 * b, 16), :] = rows(mine + b)


def join_kernel(zh_ref, own_ref, first_ref, later_ref, out_ref):
    for side in range(2):

        @pl.when(zh_ref[0] == side)
        def _():
            mine, theirs = 8 * side, 8 * (1 - side)
            for b in range(8):
                out_ref[:, mine + b, :] = own_ref[pl.ds(16 * b, 16), :]
            for y in range(4):
                out_ref[:, theirs + 2 * y, :] = first_ref[pl.ds(16 * y, 16), :]
                out_ref[:, theirs + 2 * y + 1, :] = later_ref[pl.ds(16 * y, 16), :]


def product(a, b):
    return jnp.dot(a, b, precision=HIGHEST, preferred_element_type=jnp.float32)


def across(a, b):
    return lax.dot_general(
        a, b, (((1,), (1,)), ((), ())), precision=HIGHEST, preferred_element_type=jnp.float32
    )


def gram_kernel(core_ref, table_ref, own_ref, early_ref, late_ref, gram_ref, average_ref, deviation_ref):
    other = jnp.where(core_ref[0] == 0, early_ref[...], late_ref[...])
    states = jnp.concatenate([own_ref[...], other], axis=0)
    average = jnp.sum(states, axis=0, keepdims=True) / K
    deviation = states - average
    average_ref[...] = jnp.broadcast_to(average, average_ref.shape)
    deviation_ref[...] = deviation
    weight, pull = table_ref[0:1, :], table_ref[1:2, :]
    scaled = deviation * jnp.sqrt(weight)
    gram = across(scaled, scaled)
    right = across(jnp.broadcast_to(pull - weight * average, average_ref.shape), deviation)
    gram_ref[0:128, :] = gram[:HALF, :HALF]
    gram_ref[128:256, :] = gram[:HALF, HALF:]
    gram_ref[256:384, :] = gram[HALF:, HALF:]
    gram_ref[384:392, :] = right[:, :HALF]
    gram_ref[392:400, :] = right[:, HALF:]


def two_parts(x):
    high = x.astype(jnp.bfloat16)
    return high, (x - high.astype(jnp.float32)).astype(jnp.bfloat16)


def product3(a, b):
    (ah, al), (bh, bl) = two_parts(a), two_parts(b)
    dot = functools.partial(jnp.dot, preferred_element_type=jnp.float32)
    return dot(ah, bh) + (dot(ah, bl) + dot(al, bh))


def analyse_kernel(
    core_ref, gram_ref, west_ref, east_ref, average_ref, deviation_ref, mine_ref, keep_ref, send_ref, u_ref, z_ref
):
    total = gram_ref[...] + 0.5 * (west_ref[...] + east_ref[...])
    g11, g12, g22 = total[:128], total[128:256], total[256:384]
    right = jnp.concatenate([total[384:385], total[392:393]], axis=1)
    gram = jnp.concatenate(
        [jnp.concatenate([g11, g12], axis=1), jnp.concatenate([g12.T, g22], axis=1)], axis=0
    )
    rows = lax.broadcasted_iota(jnp.int32, (K, K), 0)
    columns = lax.broadcasted_iota(jnp.int32, (K, K), 1)
    diagonal = rows == columns
    system = gram + jnp.where(diagonal, K - 1.0, 0.0)
    factor = jnp.sqrt(jnp.sum(system * system, keepdims=True) + 1e-06)
    three = jnp.where(diagonal, 3.0, 0.0)
    root = system / factor
    middle = three - root
    u_ref[...] = 0.5 * product(root, middle)
    z_ref[...] = 0.5 * middle

    def sweep(_, carry):
        root, inverse = u_ref[...], z_ref[...]
        middle = three - product(inverse, root)
        u_ref[...] = 0.5 * product(root, middle)
        z_ref[...] = 0.5 * product(middle, inverse)
        return carry

    lax.fori_loop(0, ITERS - 2, sweep, 0)
    root, inverse = u_ref[...], z_ref[...]
    inverse = 0.5 * product(three - product(inverse, root), inverse)
    inverse = inverse / jnp.sqrt(factor)
    pulled = jnp.sum(inverse * right, axis=1, keepdims=True)
    shift = jnp.sum(inverse * pulled, axis=0, keepdims=True)
    weights = math.sqrt(K - 1.0) * inverse + shift
    result = average_ref[0:1, :] + product3(weights, deviation_ref[...])
    mine_ref[...] = result[:HALF]
    quarter = HALF // 2
    for core in range(2):

        @pl.when(core_ref[0] == core)
        def _():
            keep_ref[...] = result[HALF + core * quarter :][:quarter]
            send_ref[...] = result[HALF + (1 - core) * quarter :][:quarter]


def shards(members, obs_value, obs_precision, obs_index, obs_count):
    zh, y, core = (lax.axis_index(a) for a in MEMBER)
    regions = lax.axis_size("region")
    width = members.shape[2]
    side = zh.astype(jnp.int32).reshape(1)
    which = core.astype(jnp.int32).reshape(1)

    first, own, later = call(
        split_kernel, (f32(64, width), f32(128, width), f32(64, width)), [SMEM, VMEM]
    )(side, members)

    def swap(x):
        return lax.ppermute(x, "zh", [(0, 1), (1, 0)])

    def swap_on(x, s):
        return lax.ppermute(x, ("zh", "core"), [(s, 2 + s), (2 + s, s)])

    def to_core(x, s):
        return lax.ppermute(x, "core", [(1 - s, s)])

    def over_y(x):
        return lax.all_to_all(x, "y", split_axis=0, concat_axis=0, tiled=True)

    def over_y_core(x):
        return lax.all_to_all(x, ("y", "core"), split_axis=0, concat_axis=0, tiled=True)

    def beside(x):
        found = []
        for odd in (0, 1):
            ahead = [(r, (r + 1) % regions) for r in range(odd, regions, 2)]
            found.append(lax.ppermute(x, "region", ahead + [(b, a) for a, b in ahead]))
        return found

    crossed = swap(first)
    always = obs_count[0] > 0

    def spread(later, own):
        near = over_y(later)
        far = to_core(near, 1)
        return jnp.concatenate([far, near]).reshape(HALF, width)

    def no_spread(later, own):
        return own.reshape(HALF, width)

    later = lax.cond(always, spread, no_spread, later, own)
    later_crossed = swap_on(later, 1)

    band = zh * 8 + y * 2 + core
    pick = lambda t: lax.dynamic_index_in_dim(t, band, 0, keepdims=False)
    places, observed, accuracy, filled = map(pick, (obs_index, obs_value, obs_precision, obs_count))
    slots = jnp.arange(width, dtype=jnp.int32)
    accuracy = jnp.where(slots < filled, accuracy, 0.0)
    hit = places[:, None] == slots[None, :]
    weight = jnp.sum(jnp.where(hit, accuracy[:, None], 0.0), axis=0)
    pull = jnp.sum(jnp.where(hit, (accuracy * observed)[:, None], 0.0), axis=0)
    table = jnp.stack([weight, pull])

    def gathered(crossed):
        near = over_y(crossed)
        far = to_core(near, 0)
        return jnp.concatenate([near, far]).reshape(HALF, width)

    own = lax.cond(always, over_y_core, lambda x: x, own)
    crossed, own, table = lax.optimization_barrier((crossed, own, table))
    early = lax.cond(always, gathered, lambda x: jnp.concatenate([x, x]).reshape(HALF, width), crossed)
    later_crossed, early = lax.optimization_barrier((later_crossed, early))

    gram, average, deviation = call(
        gram_kernel, (f32(400, 128), f32(8, width), f32(K, width)), [SMEM] + [VMEM] * 4
    )(which, table, own, early, later_crossed)
    west, east = beside(gram)
    mine, keep, send = call(
        analyse_kernel,
        (f32(HALF, width), f32(64, width), f32(64, width)),
        [SMEM] + [VMEM] * 5,
        scratch=[pltpu.VMEM((K, K), jnp.float32)] * 2,
    )(which, gram, west, east, average, deviation)

    got = lax.ppermute(send, "core", [(0, 1), (1, 0)])
    back_0 = swap(over_y(jnp.where(core == 0, keep, got)))
    crossing = lax.cond(always, over_y, lambda x: x, jnp.where(core == 0, got, keep))
    back_1 = swap(crossing)
    crossing, mine = lax.optimization_barrier((crossing, mine))
    mine = lax.cond(always, over_y_core, lambda x: x, mine)
    return call(join_kernel, f32(*members.shape), [SMEM] + [VMEM] * 3)(side, mine, back_0, back_1)


def solution(mesh):
    split = Mesh(
        mesh.devices.reshape(mesh.shape["region"], 2, 4, 2), ("region", "zh", "y", "core")
    )
    placed = (
        P(MEMBER, "region", None),
        P("region", None),
        P("region", None),
        P("region", None),
        P("region"),
    )
    return jax.shard_map(
        shards, mesh=split, in_specs=placed, out_specs=P(MEMBER, "region", None), check_vma=False
    )
```

```python
import functools
import math

import jax
import jax.numpy as jnp
from jax import lax
from jax.experimental import pallas as pl
from jax.experimental.pallas import tpu as pltpu
from jax.sharding import Mesh
from jax.sharding import PartitionSpec as P

K = 256
ITERS = 12
HALF = K // 2
MEMBER = ("zh", "y", "core")
HIGHEST = lax.Precision.HIGHEST
VMEM = pl.BlockSpec(memory_space=pltpu.VMEM)
SMEM = pl.BlockSpec(memory_space=pltpu.SMEM)


def call(kernel, outs, specs, scratch=(), weight=0):
    return pl.pallas_call(
        kernel,
        out_shape=outs,
        in_specs=specs,
        out_specs=jax.tree.map(lambda _: VMEM, outs),
        scratch_shapes=list(scratch),
        compiler_params=pltpu.CompilerParams(vmem_limit_bytes=24 << 20),
        cost_estimate=pl.CostEstimate(flops=weight, bytes_accessed=weight, transcendentals=0),
    )


def f32(*shape):
    return jax.ShapeDtypeStruct(shape, jnp.float32)


def split_kernel(zh_ref, x_ref, first_ref, own_ref, later_ref):
    def rows(band):
        return x_ref[:, band, :]

    for side in range(2):

        @pl.when(zh_ref[0] == side)
        def _():
            mine, theirs = 8 * side, 8 * (1 - side)
            for y in range(4):
                first_ref[pl.ds(16 * y, 16), :] = rows(theirs + 2 * y)
                later_ref[pl.ds(16 * y, 16), :] = rows(theirs + 2 * y + 1)
            for b in range(8):
                own_ref[pl.ds(16 * b, 16), :] = rows(mine + b)


def join_first_kernel(zh_ref, own_ref, first_ref, out_ref):
    for side in range(2):

        @pl.when(zh_ref[0] == side)
        def _():
            mine, theirs = 8 * side, 8 * (1 - side)
            for b in range(8):
                out_ref[:, mine + b, :] = own_ref[pl.ds(16 * b, 16), :]
            for y in range(4):
                out_ref[0:8, theirs + 2 * y, :] = first_ref[y]


def join_rest_kernel(zh_ref, rest_ref, begun_ref, out_ref):
    out_ref[...] = begun_ref[...]
    for side in range(2):

        @pl.when(zh_ref[0] == side)
        def _():
            theirs = 8 * (1 - side)
            for y in range(4):
                out_ref[8:16, theirs + 2 * y, :] = rest_ref[y, 0:8]
                out_ref[:, theirs + 2 * y + 1, :] = rest_ref[y, 8:24]


def product(a, b):
    return jnp.dot(a, b, precision=HIGHEST, preferred_element_type=jnp.float32)


def across(a, b):
    return lax.dot_general(
        a, b, (((1,), (1,)), ((), ())), precision=HIGHEST, preferred_element_type=jnp.float32
    )


def gram_kernel(core_ref, table_ref, own_ref, early_ref, late_ref, gram_ref, average_ref, deviation_ref):
    other = jnp.where(core_ref[0] == 0, early_ref[...], late_ref[...])
    states = jnp.concatenate([own_ref[...], other], axis=0)
    average = jnp.sum(states, axis=0, keepdims=True) / K
    deviation = states - average
    average_ref[...] = jnp.broadcast_to(average, average_ref.shape)
    deviation_ref[...] = deviation
    weight, pull = table_ref[0:1, :], table_ref[1:2, :]
    scaled = deviation * jnp.sqrt(weight)
    gram = across(scaled, scaled)
    right = across(jnp.broadcast_to(pull - weight * average, average_ref.shape), deviation)
    gram_ref[0:128, :] = gram[:HALF, :HALF]
    gram_ref[128:256, :] = gram[:HALF, HALF:]
    gram_ref[256:384, :] = gram[HALF:, HALF:]
    gram_ref[384:392, :] = right[:, :HALF]
    gram_ref[392:400, :] = right[:, HALF:]


def two_parts(x):
    high = x.astype(jnp.bfloat16)
    return high, (x - high.astype(jnp.float32)).astype(jnp.bfloat16)


def product3(a, b):
    (ah, al), (bh, bl) = two_parts(a), two_parts(b)
    dot = functools.partial(jnp.dot, preferred_element_type=jnp.float32)
    return dot(ah, bh) + (dot(ah, bl) + dot(al, bh))


def analyse_kernel(
    core_ref, gram_ref, west_ref, east_ref, average_ref, deviation_ref, mine_ref, keep_ref, send_ref, u_ref, z_ref
):
    total = gram_ref[...] + 0.5 * (west_ref[...] + east_ref[...])
    g11, g12, g22 = total[:128], total[128:256], total[256:384]
    right = jnp.concatenate([total[384:385], total[392:393]], axis=1)
    gram = jnp.concatenate(
        [jnp.concatenate([g11, g12], axis=1), jnp.concatenate([g12.T, g22], axis=1)], axis=0
    )
    rows = lax.broadcasted_iota(jnp.int32, (K, K), 0)
    columns = lax.broadcasted_iota(jnp.int32, (K, K), 1)
    diagonal = rows == columns
    system = gram + jnp.where(diagonal, K - 1.0, 0.0)
    factor = jnp.sqrt(jnp.sum(system * system, keepdims=True) + 1e-06)
    three = jnp.where(diagonal, 3.0, 0.0)
    root = system / factor
    middle = three - root
    u_ref[...] = 0.5 * product(root, middle)
    z_ref[...] = 0.5 * middle

    def sweep(_, carry):
        root, inverse = u_ref[...], z_ref[...]
        middle = three - product(inverse, root)
        u_ref[...] = 0.5 * product(root, middle)
        z_ref[...] = 0.5 * product(middle, inverse)
        return carry

    lax.fori_loop(0, ITERS - 2, sweep, 0)
    root, inverse = u_ref[...], z_ref[...]
    inverse = 0.5 * product(three - product(inverse, root), inverse)
    inverse = inverse / jnp.sqrt(factor)
    pulled = jnp.sum(inverse * right, axis=1, keepdims=True)
    shift = jnp.sum(inverse * pulled, axis=0, keepdims=True)
    weights = math.sqrt(K - 1.0) * inverse + shift
    result = average_ref[0:1, :] + product3(weights, deviation_ref[...])
    mine_ref[...] = result[:HALF]
    quarter = HALF // 2
    for core in range(2):

        @pl.when(core_ref[0] == core)
        def _():
            keep_ref[...] = result[HALF + core * quarter :][:quarter]
            send_ref[...] = result[HALF + (1 - core) * quarter :][:quarter]


def shards(members, obs_value, obs_precision, obs_index, obs_count):
    zh, y, core = (lax.axis_index(a) for a in MEMBER)
    regions = lax.axis_size("region")
    width = members.shape[2]
    side = zh.astype(jnp.int32).reshape(1)
    which = core.astype(jnp.int32).reshape(1)

    first, own, later = call(
        split_kernel, (f32(64, width), f32(128, width), f32(64, width)), [SMEM, VMEM]
    )(side, members)

    def swap(x):
        return lax.ppermute(x, "zh", [(0, 1), (1, 0)])

    def swap_on(x, s):
        return lax.ppermute(x, ("zh", "core"), [(s, 2 + s), (2 + s, s)])

    def to_core(x, s):
        return lax.ppermute(x, "core", [(1 - s, s)])

    def over_y(x):
        return lax.all_to_all(x, "y", split_axis=0, concat_axis=0, tiled=True)

    def over_y_core(x):
        return lax.all_to_all(x, ("y", "core"), split_axis=0, concat_axis=0, tiled=True)

    def beside(x):
        found = []
        for odd in (0, 1):
            ahead = [(r, (r + 1) % regions) for r in range(odd, regions, 2)]
            found.append(lax.ppermute(x, "region", ahead + [(b, a) for a, b in ahead]))
        return found

    crossed = swap(first)
    always = obs_count[0] > 0

    def spread(later, own):
        near = over_y(later)
        far = to_core(near, 1)
        return jnp.concatenate([far, near]).reshape(HALF, width)

    def no_spread(later, own):
        return own.reshape(HALF, width)

    later = lax.cond(always, spread, no_spread, later, own)
    later_crossed = swap_on(later, 1)

    band = zh * 8 + y * 2 + core
    pick = lambda t: lax.dynamic_index_in_dim(t, band, 0, keepdims=False)
    places, observed, accuracy, filled = map(pick, (obs_index, obs_value, obs_precision, obs_count))
    slots = jnp.arange(width, dtype=jnp.int32)
    accuracy = jnp.where(slots < filled, accuracy, 0.0)
    hit = places[:, None] == slots[None, :]
    weight = jnp.sum(jnp.where(hit, accuracy[:, None], 0.0), axis=0)
    pull = jnp.sum(jnp.where(hit, (accuracy * observed)[:, None], 0.0), axis=0)
    table = jnp.stack([weight, pull])

    def gathered(crossed):
        near = over_y(crossed)
        far = to_core(near, 0)
        return jnp.concatenate([near, far]).reshape(HALF, width)

    own = lax.cond(always, over_y_core, lambda x: x, own)
    crossed, own, table = lax.optimization_barrier((crossed, own, table))
    early = lax.cond(always, gathered, lambda x: jnp.concatenate([x, x]).reshape(HALF, width), crossed)
    later_crossed, early = lax.optimization_barrier((later_crossed, early))

    gram, average, deviation = call(
        gram_kernel, (f32(400, 128), f32(8, width), f32(K, width)), [SMEM] + [VMEM] * 4
    )(which, table, own, early, later_crossed)
    west, east = beside(gram)
    mine, keep, send = call(
        analyse_kernel,
        (f32(HALF, width), f32(64, width), f32(64, width)),
        [SMEM] + [VMEM] * 5,
        scratch=[pltpu.VMEM((K, K), jnp.float32)] * 2,
    )(which, gram, west, east, average, deviation)

    got = lax.ppermute(send, "core", [(0, 1), (1, 0)])
    lower = jnp.where(core == 0, keep, got).reshape(4, 16, width)
    upper = jnp.where(core == 0, got, keep).reshape(4, 16, width)
    back_0 = swap(lower[:, :8])
    crossing = lax.cond(
        always,
        lambda x, y: over_y(jnp.concatenate([x, y], axis=1)),
        lambda x, y: jnp.concatenate([y, x], axis=1),
        lower[:, 8:],
        upper,
    )
    back_1 = swap(crossing)
    crossing, mine = lax.optimization_barrier((crossing, mine))
    mine = lax.cond(always, over_y_core, lambda x: x, mine)
    back_0, mine = lax.optimization_barrier((back_0, mine))
    back_0 = lax.cond(always, over_y, lambda x: x, back_0)
    out = call(join_first_kernel, f32(*members.shape), [SMEM] + [VMEM] * 2, weight=1 << 36)(side, mine, back_0)
    return call(join_rest_kernel, f32(*members.shape), [SMEM] + [VMEM] * 2)(side, back_1, out)


def solution(mesh):
    split = Mesh(
        mesh.devices.reshape(mesh.shape["region"], 2, 4, 2), ("region", "zh", "y", "core")
    )
    placed = (
        P(MEMBER, "region", None),
        P("region", None),
        P("region", None),
        P("region", None),
        P("region"),
    )
    return jax.shard_map(
        shards, mesh=split, in_specs=placed, out_specs=P(MEMBER, "region", None), check_vma=False
    )
```

```python
import functools
import math

import jax
import jax.numpy as jnp
from jax import lax
from jax.experimental import pallas as pl
from jax.experimental.pallas import tpu as pltpu
from jax.sharding import Mesh
from jax.sharding import PartitionSpec as P

K = 256
ITERS = 12
HALF = K // 2
MEMBER = ("zh", "y", "core")
HIGHEST = lax.Precision.HIGHEST
VMEM = pl.BlockSpec(memory_space=pltpu.VMEM)
SMEM = pl.BlockSpec(memory_space=pltpu.SMEM)


def call(kernel, outs, specs, scratch=()):
    return pl.pallas_call(
        kernel,
        out_shape=outs,
        in_specs=specs,
        out_specs=jax.tree.map(lambda _: VMEM, outs),
        scratch_shapes=list(scratch),
        compiler_params=pltpu.CompilerParams(vmem_limit_bytes=24 << 20),
        cost_estimate=pl.CostEstimate(flops=0, bytes_accessed=0, transcendentals=0),
    )


def f32(*shape):
    return jax.ShapeDtypeStruct(shape, jnp.float32)


def split_kernel(zh_ref, x_ref, own_ref, other_ref):
    for side in range(2):

        @pl.when(zh_ref[0] == side)
        def _():
            for b in range(8):
                other_ref[pl.ds(16 * b, 16), :] = x_ref[:, 8 * (1 - side) + b, :]
                own_ref[pl.ds(16 * b, 16), :] = x_ref[:, 8 * side + b, :]


def join_kernel(zh_ref, own_ref, first_ref, later_ref, out_ref):
    for side in range(2):

        @pl.when(zh_ref[0] == side)
        def _():
            mine, theirs = 8 * side, 8 * (1 - side)
            for b in range(8):
                out_ref[:, mine + b, :] = own_ref[pl.ds(16 * b, 16), :]
            for y in range(4):
                out_ref[:, theirs + 2 * y, :] = first_ref[pl.ds(16 * y, 16), :]
                out_ref[:, theirs + 2 * y + 1, :] = later_ref[pl.ds(16 * y, 16), :]


def product(a, b):
    return jnp.dot(a, b, precision=HIGHEST, preferred_element_type=jnp.float32)


def across(a, b):
    return lax.dot_general(
        a, b, (((1,), (1,)), ((), ())), precision=HIGHEST, preferred_element_type=jnp.float32
    )


def gram_kernel(table_ref, own_ref, other_ref, gram_ref, average_ref, deviation_ref):
    other = [other_ref[pl.ds(16 * (2 * y + core), 16), :] for core in range(2) for y in range(4)]
    states = jnp.concatenate([own_ref[...]] + other, axis=0)
    average = jnp.sum(states, axis=0, keepdims=True) / K
    deviation = states - average
    average_ref[...] = jnp.broadcast_to(average, average_ref.shape)
    deviation_ref[...] = deviation
    weight, pull = table_ref[0:1, :], table_ref[1:2, :]
    scaled = deviation * jnp.sqrt(weight)
    gram = across(scaled, scaled)
    right = across(jnp.broadcast_to(pull - weight * average, average_ref.shape), deviation)
    gram_ref[0:128, :] = gram[:HALF, :HALF]
    gram_ref[128:256, :] = gram[:HALF, HALF:]
    gram_ref[256:384, :] = gram[HALF:, HALF:]
    gram_ref[384:392, :] = right[:, :HALF]
    gram_ref[392:400, :] = right[:, HALF:]


def two_parts(x):
    high = x.astype(jnp.bfloat16)
    return high, (x - high.astype(jnp.float32)).astype(jnp.bfloat16)


def product3(a, b):
    (ah, al), (bh, bl) = two_parts(a), two_parts(b)
    dot = functools.partial(jnp.dot, preferred_element_type=jnp.float32)
    return dot(ah, bh) + (dot(ah, bl) + dot(al, bh))


def analyse_kernel(
    core_ref, gram_ref, west_ref, east_ref, average_ref, deviation_ref, mine_ref, keep_ref, send_ref, u_ref, z_ref
):
    total = gram_ref[...] + 0.5 * (west_ref[...] + east_ref[...])
    g11, g12, g22 = total[:128], total[128:256], total[256:384]
    right = jnp.concatenate([total[384:385], total[392:393]], axis=1)
    gram = jnp.concatenate(
        [jnp.concatenate([g11, g12], axis=1), jnp.concatenate([g12.T, g22], axis=1)], axis=0
    )
    rows = lax.broadcasted_iota(jnp.int32, (K, K), 0)
    columns = lax.broadcasted_iota(jnp.int32, (K, K), 1)
    diagonal = rows == columns
    system = gram + jnp.where(diagonal, K - 1.0, 0.0)
    factor = jnp.sqrt(jnp.sum(system * system, keepdims=True) + 1e-06)
    three = jnp.where(diagonal, 3.0, 0.0)
    root = system / factor
    middle = three - root
    u_ref[...] = 0.5 * product(root, middle)
    z_ref[...] = 0.5 * middle

    def sweep(_, carry):
        root, inverse = u_ref[...], z_ref[...]
        middle = three - product(inverse, root)
        u_ref[...] = 0.5 * product(root, middle)
        z_ref[...] = 0.5 * product(middle, inverse)
        return carry

    lax.fori_loop(0, ITERS - 2, sweep, 0)
    root, inverse = u_ref[...], z_ref[...]
    inverse = 0.5 * product(three - product(inverse, root), inverse)
    inverse = inverse / jnp.sqrt(factor)
    pulled = jnp.sum(inverse * right, axis=1, keepdims=True)
    shift = jnp.sum(inverse * pulled, axis=0, keepdims=True)
    weights = math.sqrt(K - 1.0) * inverse + shift
    result = average_ref[0:1, :] + product3(weights, deviation_ref[...])
    mine_ref[...] = result[:HALF]
    quarter = HALF // 2
    for core in range(2):

        @pl.when(core_ref[0] == core)
        def _():
            keep_ref[...] = result[HALF + core * quarter :][:quarter]
            send_ref[...] = result[HALF + (1 - core) * quarter :][:quarter]


def shards(members, obs_value, obs_precision, obs_index, obs_count):
    zh, y, core = (lax.axis_index(a) for a in MEMBER)
    regions = lax.axis_size("region")
    width = members.shape[2]
    side = zh.astype(jnp.int32).reshape(1)
    which = core.astype(jnp.int32).reshape(1)

    own, other = call(split_kernel, (f32(HALF, width), f32(HALF, width)), [SMEM, VMEM])(side, members)

    def swap(x):
        return lax.ppermute(x, "zh", [(0, 1), (1, 0)])

    def over_y(x):
        return lax.all_to_all(x, "y", split_axis=0, concat_axis=0, tiled=True)

    def over_y_core(x):
        return lax.all_to_all(x, ("y", "core"), split_axis=0, concat_axis=0, tiled=True)

    def beside(x):
        found = []
        for odd in (0, 1):
            ahead = [(r, (r + 1) % regions) for r in range(odd, regions, 2)]
            found.append(lax.ppermute(x, "region", ahead + [(b, a) for a, b in ahead]))
        return found

    crossed = swap(other)
    always = obs_count[0] > 0

    band = zh * 8 + y * 2 + core
    pick = lambda t: lax.dynamic_index_in_dim(t, band, 0, keepdims=False)
    places, observed, accuracy, filled = map(pick, (obs_index, obs_value, obs_precision, obs_count))
    slots = jnp.arange(width, dtype=jnp.int32)
    accuracy = jnp.where(slots < filled, accuracy, 0.0)
    hit = places[:, None] == slots[None, :]
    weight = jnp.sum(jnp.where(hit, accuracy[:, None], 0.0), axis=0)
    pull = jnp.sum(jnp.where(hit, (accuracy * observed)[:, None], 0.0), axis=0)
    table = jnp.stack([weight, pull])

    own = lax.cond(always, over_y_core, lambda x: x, own)
    crossed, own, table = lax.optimization_barrier((crossed, own, table))
    other = over_y_core(crossed)

    gram, average, deviation = call(
        gram_kernel, (f32(400, 128), f32(8, width), f32(K, width)), [VMEM] * 3
    )(table, own, other)
    west, east = beside(gram)
    mine, keep, send = call(
        analyse_kernel,
        (f32(HALF, width), f32(64, width), f32(64, width)),
        [SMEM] + [VMEM] * 5,
        scratch=[pltpu.VMEM((K, K), jnp.float32)] * 2,
    )(which, gram, west, east, average, deviation)

    got = lax.ppermute(send, "core", [(0, 1), (1, 0)])
    back_0 = swap(jnp.where(core == 0, keep, got))
    crossing = lax.cond(always, over_y, lambda x: x, jnp.where(core == 0, got, keep))
    back_1 = swap(crossing)
    crossing, mine = lax.optimization_barrier((crossing, mine))
    mine = lax.cond(always, over_y_core, lambda x: x, mine)
    back_0, mine = lax.optimization_barrier((back_0, mine))
    back_0 = lax.cond(always, over_y, lambda x: x, back_0)
    return call(join_kernel, f32(*members.shape), [SMEM] + [VMEM] * 3)(side, mine, back_0, back_1)


def solution(mesh):
    split = Mesh(
        mesh.devices.reshape(mesh.shape["region"], 2, 4, 2), ("region", "zh", "y", "core")
    )
    placed = (
        P(MEMBER, "region", None),
        P("region", None),
        P("region", None),
        P("region", None),
        P("region"),
    )
    return jax.shard_map(
        shards, mesh=split, in_specs=placed, out_specs=P(MEMBER, "region", None), check_vma=False
    )
```
